32 devices in a mesh: kpt: 2 (over y), state: 8 (over z, x), dom: 2 (over core).
Axes of the slice: x: 2, y: 2, z: 4, core: 2. Of those that a mesh axis runs over, the one named last changes fastest.
Arguments:
- previous: float32 [1024, 16, 4, 128], P(('kpt', 'state'), 'dom'), parts along dimension 0, may hold values from -6 to 6
- current: float32 [1024, 16, 4, 128], P(('kpt', 'state'), 'dom'), parts along dimension 0, may hold values from -6 to 6
- potential: float32 [16, 4, 128], P('dom'), may hold values from -3 to 1
- degree: int32 [1024], P(('kpt', 'state')), parts along dimension 0, may hold values from 1 to 16
- panel_index: int32 [2], P('kpt'), parts along dimension 0, may hold values from 0 to 7
Outputs:
- filtered: float32 [1024, 16, 4, 128], P(('kpt', 'state'), 'dom'), parts along dimension 0
- margin: float32 [128, 512], P(('kpt', 'dom'), 'state'), parts along dimension 0
The draws below stay inside these ranges and needn't reach their ends.
There are 2 independent parts, one for each index of `kpt`. The reference program is written for one: setup_inputs(seed, part) draws one part's arguments, and reference() takes and returns one part's arrays. A program takes and returns all parts, laid end to end along the dimension named above; an argument that names none is the same for every part. Nothing has to cross between parts.
All inputs are finite; a program needn't handle non-finite values.
Results may differ from the reference program's by a relative error of at most 0.00011.
Values sent between devices are 32-bit elements; how exact they have to be, the bound alone decides.
A program may use at most 128 MiB of HBM per device.

```python
import jax
import jax.numpy as jnp
from jax import lax

ORB_DEV = 64
ORBITALS = 512
PANELS = 8
NY = 4
NZ = 128
NX = 16


def plant(entries, own_key, least, top_value):
    dims = entries.shape
    spot = [jax.random.randint(jax.random.fold_in(own_key, axis), (), 0, dims[axis]) for axis in range(len(dims))]
    entries = entries.at[tuple(spot)].set(least)
    longest = dims.index(max(dims))
    spot[longest] = (spot[longest] + 1) % dims[longest]
    return entries.at[tuple(spot)].set(top_value)


def levels(rng, extent, cuts, low, top_value):
    gain, own = 1.0, jax.random.fold_in(rng, 6)
    for position, parts in cuts:
        steps = jnp.exp(jax.random.uniform(jax.random.fold_in(own, position), (parts,), jnp.float32, low / len(cuts), top_value / len(cuts)))
        gain = gain * jnp.repeat(steps, extent[position] // parts).reshape([-1 if axis == position else 1 for axis in range(len(extent))])
    return gain


def scatter_about(stream_key, extent, width, reach, cuts=(), dtype=jnp.bfloat16):
    values = width * jax.random.normal(stream_key, extent, jnp.float32)
    if cuts:
        values = values * levels(stream_key, extent, cuts, -0.22, 0.18)
    return jnp.clip(values, -reach, reach).astype(dtype)


def setup_inputs(seed: int = 0, part: int = 0) -> dict:
    splits = jax.random.split(jax.random.key(seed), 6)
    own_keys = jax.random.split(jax.random.fold_in(splits[5], part), 6)
    return {
        "previous": scatter_about(own_keys[0], (ORBITALS, NX, NY, NZ), 1.0, 6.0, ((0, 8), (1, 2)), jnp.float32),
        "current": scatter_about(own_keys[1], (ORBITALS, NX, NY, NZ), 1.0, 6.0, ((0, 8), (1, 2)), jnp.float32),
        "potential": jnp.clip(-3.0 + 4.0 * jax.random.uniform(splits[2], (NX, NY, NZ), jnp.float32) ** levels(splits[2], (NX, NY, NZ), ((0, 2),), -0.2, 0.2), -3.0, 1.0),
        "degree": plant(jax.random.randint(own_keys[3], (ORBITALS,), 1, 17), jax.random.fold_in(own_keys[3], 1), 1, 16).astype(jnp.int32),
        "panel_index": jax.random.randint(own_keys[4], (1,), 0, PANELS).astype(jnp.int32),
    }


stencil_weights = (-5369.0 / 1800.0, 12.0 / 7.0, -15.0 / 56.0, 10.0 / 189.0, -1.0 / 112.0, 2.0 / 1925.0, -1.0 / 16632.0)
spectrum_center = 8.0
spectrum_half = 8.0
first_ratio = 8.0 / (-0.5 - 8.0)
inverse_two = 2.0 / first_ratio


def sigma_table(degree):
    sigma_now = jnp.full(degree.shape, first_ratio, jnp.float32)
    for repeat in range(1, 16):
        sigma_now = jnp.where(repeat < degree, 1.0 / (inverse_two - sigma_now), sigma_now)
    sigma_next = 1.0 / (inverse_two - sigma_now)
    sigma_after = 1.0 / (inverse_two - sigma_next)
    return sigma_now, sigma_next, sigma_after


def laplace_local(orbital):
    running = 3.0 * stencil_weights[0] * orbital
    for offset in range(1, 7):
        beside = jnp.roll(orbital, offset, 1) + jnp.roll(orbital, -offset, 1)
        beside = beside + jnp.roll(orbital, offset, 2) + jnp.roll(orbital, -offset, 2)
        beside = beside + jnp.roll(orbital, offset, 3) + jnp.roll(orbital, -offset, 3)
        running = running + stencil_weights[offset] * beside
    return running


def advance(older, newer, applied, potential, sigma_low, sigma_high):
    hamilton = -0.5 * applied + potential * newer
    return (2.0 * sigma_high / spectrum_half) * (hamilton - spectrum_center * newer) - sigma_low * sigma_high * older


def reference(previous, current, potential, degree, panel_index):
    sigma_now, sigma_next, sigma_after = sigma_table(degree)
    shape_blocks = (PANELS, ORB_DEV, 1, 1, 1)

    def one_block(pieces):
        older, newer, first, second, third = pieces
        middle = advance(older, newer, laplace_local(newer), potential, first, second)
        return advance(newer, middle, laplace_local(middle), potential, second, third)

    filtered = lax.map(one_block, (previous.reshape(PANELS, ORB_DEV, NX, NY, NZ), current.reshape(PANELS, ORB_DEV, NX, NY, NZ), sigma_now.reshape(shape_blocks), sigma_next.reshape(shape_blocks), sigma_after.reshape(shape_blocks)))
    filtered = filtered.reshape(ORBITALS, NX, NY, NZ)
    start_row = (panel_index[0] * ORB_DEV).astype(jnp.int32)
    panel_rows = lax.dynamic_slice_in_dim(filtered, start_row, ORB_DEV, 0)
    summed = jnp.dot(panel_rows.reshape(ORB_DEV, -1), filtered.reshape(ORBITALS, -1).T, precision=lax.Precision.HIGHEST, preferred_element_type=jnp.float32)
    margin = summed / (NX * NY * NZ)
    return filtered, margin
```

```python
import functools

import jax
import jax.numpy as jnp
import numpy as np
from jax import lax
from jax.experimental import pallas as pl
from jax.experimental.pallas import tpu as pltpu
from jax.sharding import PartitionSpec as P

stencil_weights = (
    -5369.0 / 1800.0,
    12.0 / 7.0,
    -15.0 / 56.0,
    10.0 / 189.0,
    -1.0 / 112.0,
    2.0 / 1925.0,
    -1.0 / 16632.0,
)
spectrum_center = 8.0
spectrum_half = 8.0
first_ratio = 8.0 / (-0.5 - 8.0)
inverse_two = 2.0 / first_ratio
GROUP = 8


def sigma_table(degree):
    sigma_now = jnp.full(degree.shape, first_ratio, jnp.float32)
    for repeat in range(1, 16):
        sigma_now = jnp.where(repeat < degree, 1.0 / (inverse_two - sigma_now), sigma_now)
    sigma_next = 1.0 / (inverse_two - sigma_now)
    sigma_after = 1.0 / (inverse_two - sigma_next)
    return (sigma_now, sigma_next, sigma_after)


def circulant_row(length):
    row = np.zeros(length)
    for m in range(1, len(stencil_weights)):
        row[m % length] += -0.5 * stencil_weights[m]
        row[-m % length] += -0.5 * stencil_weights[m]
    return row


def z_matrix(length):
    row = circulant_row(length)
    full = np.stack([np.roll(row, i) for i in range(length)]).astype(np.float32)
    high = full.astype(jnp.bfloat16)
    low = (full - high.astype(np.float32)).astype(jnp.bfloat16)
    zero = np.zeros_like(high)
    return np.block([[high, low], [high, zero]])


def split(value):
    high = value.astype(jnp.bfloat16)
    low = (value - high.astype(jnp.float32)).astype(jnp.bfloat16)
    return high, low


def kernel(
    sizes,
    root_ref, cur, prev, pot, coef, zmat, out, margin,
    curf, prevf, potf, potb, tcur, tmid, zterm, full, own, slots, panel, parted, partial, other,
    in_local, in_send, in_recv, back_local, back_send, back_recv,
    rs_send, rs_recv, ag_send, ag_recv, piece_sem, out_sem, sum_send, sum_recv,
):
    orbs, nx, ny, nz, states = sizes
    rows = nx // 2 * ny
    half = orbs // 2 * rows
    piece = orbs // states * rows
    dom, state = lax.axis_index("dom"), lax.axis_index("state")
    mate = 1 - dom

    barrier = pltpu.get_barrier_semaphore()
    pl.semaphore_signal(barrier, 1, device_id={"dom": mate}, device_id_type=pl.DeviceIdType.MESH)

    def greet(k, carry):
        pl.semaphore_signal(
            barrier, 1, device_id={"state": lax.rem(state + k, states)}, device_id_type=pl.DeviceIdType.MESH
        )
        return carry

    lax.fori_loop(1, states, greet, 0)
    pl.semaphore_wait(barrier, states)

    coming = []
    spans = ((cur, curf, half), (prev, prevf, half))
    for i, (source, target, size) in enumerate(spans):
        here = target.at[pl.ds(dom * size, size)]
        coming.append(pltpu.make_async_copy(source.at[pl.ds(dom * size, size)], here, in_local.at[i]))
        coming.append(
            pltpu.make_async_remote_copy(
                source.at[pl.ds(mate * size, size)], here, in_send.at[i], in_recv.at[i],
                device_id={"dom": mate}, device_id_type=pl.DeviceIdType.MESH,
            )
        )
    here = potf.at[pl.ds(dom * rows, rows)]
    coming.append(pltpu.make_async_copy(pot, here, in_local.at[2]))
    coming.append(
        pltpu.make_async_remote_copy(
            pot, here, in_send.at[2], in_recv.at[2], device_id={"dom": mate}, device_id_type=pl.DeviceIdType.MESH
        )
    )
    for copy in coming:
        copy.start()
    for copy in coming:
        copy.wait()
    for r in range(2 * rows):
        potb[r] = jnp.broadcast_to(potf[pl.ds(r, 1), :], (GROUP, nz))

    cx, cy = circulant_row(nx), circulant_row(ny)
    centre = -0.5 * 3.0 * stencil_weights[0] + cx[0] + cy[0] - spectrum_center

    def shifted_sum(source, x):
        mid = source[pl.ds(x * ny, ny)]
        acc = zterm[pl.ds(x * ny, ny)] + (centre + potb[pl.ds(x * ny, ny)]) * mid
        for s in range(1, ny // 2 + 1):
            if cy[s]:
                beside = jnp.concatenate([mid[s:], mid[:s]], 0)
                if 2 * s != ny:
                    beside = beside + jnp.concatenate([mid[ny - s:], mid[: ny - s]], 0)
                acc = acc + np.float32(cy[s]) * beside
        for s in range(1, nx // 2 + 1):
            if cx[s]:
                beside = source[pl.ds((x + s) % nx * ny, ny)]
                if 2 * s != nx:
                    beside = beside + source[pl.ds((x - s) % nx * ny, ny)]
                acc = acc + np.float32(cx[s]) * beside
        return acc

    def z_pass(source):
        high, low = split(source[...].reshape(nx * ny * GROUP, nz))
        both = jnp.dot(jnp.concatenate([high, low], 1), zmat[...], preferred_element_type=jnp.float32)
        zterm[...] = (both[:, :nz] + both[:, nz:]).reshape(nx * ny, GROUP, nz)

    def spot(x, y, g):
        slab, r = x // (nx // 2), x % (nx // 2) * ny + y
        return pl.ds(slab * half + g * (GROUP * rows) + r, GROUP, stride=rows)

    def one_group(g, carry):
        mine = pl.ds(dom * (orbs // 2) + g * GROUP, GROUP)
        for x in range(nx):
            for y in range(ny):
                tcur[x * ny + y] = curf[spot(x, y, g), :]
        z_pass(tcur)
        c1, d1 = coef[0, mine], coef[1, mine]
        for x in range(nx):
            acc = shifted_sum(tcur, x)
            for y in range(ny):
                tmid[x * ny + y] = c1 * acc[y] - d1 * prevf[spot(x, y, g), :]
        z_pass(tmid)
        c2, d2 = coef[2, mine], coef[3, mine]
        for x in range(nx):
            acc = shifted_sum(tmid, x)
            for y in range(ny):
                full[spot(x, y, g), :] = c2 * acc[y] - d2 * tcur[x * ny + y]
        return carry

    lax.fori_loop(0, orbs // 2 // GROUP, one_group, 0)

    landing = own.at[pl.ds(dom * half, half)]
    keep = pltpu.make_async_copy(full.at[pl.ds(dom * half, half)], landing, back_local)
    back = pltpu.make_async_remote_copy(
        full.at[pl.ds(mate * half, half)], landing, back_send, back_recv,
        device_id={"dom": mate}, device_id_type=pl.DeviceIdType.MESH,
    )
    keep.start()
    back.start()
    keep.wait()
    back.wait()
    write = pltpu.make_async_copy(own, out, out_sem)
    write.start()

    def scatter(k):
        to = lax.rem(state + k, states)
        return pltpu.make_async_remote_copy(
            own.at[pl.ds(to * piece, piece)], slots.at[state], rs_send.at[to], rs_recv.at[state],
            device_id={"state": to}, device_id_type=pl.DeviceIdType.MESH,
        )

    def scatter_in(k):
        source = lax.rem(state + k, states)
        return pltpu.make_async_remote_copy(
            own.at[pl.ds(source * piece, piece)], slots.at[source], rs_send.at[source], rs_recv.at[source],
            device_id={"state": source}, device_id_type=pl.DeviceIdType.MESH,
        )

    def gather(k):
        to = lax.rem(state + k, states)
        mine = panel.at[pl.ds(state * piece, piece)]
        return pltpu.make_async_remote_copy(
            mine, mine, ag_send.at[to], ag_recv.at[state],
            device_id={"state": to}, device_id_type=pl.DeviceIdType.MESH,
        )

    def gather_in(k):
        source = lax.rem(state + k, states)
        theirs = panel.at[pl.ds(source * piece, piece)]
        return pltpu.make_async_remote_copy(
            theirs, theirs, ag_send.at[source], ag_recv.at[source],
            device_id={"state": source}, device_id_type=pl.DeviceIdType.MESH,
        )

    def each(action):
        def step(k, carry):
            action(k)
            return carry

        lax.fori_loop(1, states, step, 0)

    each(lambda k: scatter(k).start())
    keep = pltpu.make_async_copy(own.at[pl.ds(state * piece, piece)], slots.at[state], piece_sem)
    keep.start()

    for r in range(rows):
        high, low = split(own[pl.ds(r, orbs, stride=rows), :])
        parted[r] = jnp.concatenate([high, high, low], 1)

    keep.wait()
    each(lambda k: scatter_in(k).wait_recv())
    panel[pl.ds(state * piece, piece)] = slots[root_ref[0]]
    each(lambda k: gather(k).start())
    each(lambda k: gather_in(k).wait_recv())

    total = jnp.zeros((orbs, orbs), jnp.float32)
    for r in range(rows):
        high, low = split(panel[pl.ds(r, orbs, stride=rows), :])
        total = total + lax.dot_general(
            jnp.concatenate([high, low, high], 1), parted[r], (((1,), (1,)), ((), ())),
            preferred_element_type=jnp.float32,
        )
    partial[:, :orbs] = total * np.float32(1.0 / (nx * ny * nz))
    share = orbs // 2
    swap = pltpu.make_async_remote_copy(
        partial.at[pl.ds(mate * share, share)], other, sum_send, sum_recv,
        device_id={"dom": mate}, device_id_type=pl.DeviceIdType.MESH,
    )
    swap.start()
    swap.wait()
    margin[...] = partial[pl.ds(dom * share, share), :orbs] + other[:, :orbs]

    each(lambda k: scatter(k).wait_send())
    each(lambda k: gather(k).wait_send())
    write.wait()


def on_device(mesh, previous, current, potential, degree, panel_index):
    orbs, planes, ny, nz = previous.shape
    states = mesh.shape["state"]
    nx = planes * mesh.shape["dom"]
    rows = planes * ny
    sigma_now, sigma_next, sigma_after = sigma_table(degree)
    table = jnp.stack(
        [
            2.0 * sigma_next / spectrum_half,
            sigma_now * sigma_next,
            2.0 * sigma_after / spectrum_half,
            sigma_next * sigma_after,
        ]
    )
    coef = jnp.broadcast_to(table[:, :, None], (4, orbs, nz))
    zmat = jnp.asarray(z_matrix(nz))
    vmem, anyspace = pl.BlockSpec(memory_space=pltpu.VMEM), pl.BlockSpec(memory_space=pl.ANY)
    f32, bf16 = jnp.float32, jnp.bfloat16
    piece = orbs // states * rows
    dma = pltpu.SemaphoreType.DMA
    filtered, margin = pl.pallas_call(
        functools.partial(kernel, (orbs, nx, ny, nz, states)),
        out_shape=(
            jax.ShapeDtypeStruct((orbs * rows, nz), f32),
            jax.ShapeDtypeStruct((orbs // 2, orbs), f32),
        ),
        in_specs=[pl.BlockSpec(memory_space=pltpu.SMEM), anyspace, anyspace, anyspace, vmem, vmem],
        out_specs=(anyspace, vmem),
        scratch_shapes=[
            pltpu.VMEM((orbs * rows, nz), f32),
            pltpu.VMEM((orbs * rows, nz), f32),
            pltpu.VMEM((nx * ny, nz), f32),
            pltpu.VMEM((nx * ny, GROUP, nz), f32),
            pltpu.VMEM((nx * ny, GROUP, nz), f32),
            pltpu.VMEM((nx * ny, GROUP, nz), f32),
            pltpu.VMEM((nx * ny, GROUP, nz), f32),
            pltpu.VMEM((orbs * rows, nz), f32),
            pltpu.VMEM((orbs * rows, nz), f32),
            pltpu.VMEM((states, piece, nz), f32),
            pltpu.VMEM((orbs * rows, nz), f32),
            pltpu.VMEM((rows, orbs, 3 * nz), bf16),
            pltpu.VMEM((orbs, 128), f32),
            pltpu.VMEM((orbs // 2, 128), f32),
            dma((3,)), dma((3,)), dma((3,)), dma, dma, dma,
            dma((states,)), dma((states,)), dma((states,)), dma((states,)),
            dma, dma, dma, dma,
        ],
        compiler_params=pltpu.CompilerParams(
            collective_id=0, has_side_effects=True, vmem_limit_bytes=40 * 1024 * 1024
        ),
    )(
        panel_index,
        current.reshape(orbs * rows, nz),
        previous.reshape(orbs * rows, nz),
        potential.reshape(rows, nz),
        coef,
        zmat,
    )
    return filtered.reshape(previous.shape), margin


def solution(mesh):
    return jax.shard_map(
        functools.partial(on_device, mesh),
        mesh=mesh,
        in_specs=(
            P(("kpt", "state"), "dom", None, None),
            P(("kpt", "state"), "dom", None, None),
            P("dom", None, None),
            P(("kpt", "state")),
            P("kpt"),
        ),
        out_specs=(P(("kpt", "state"), "dom", None, None), P(("kpt", "dom"), "state")),
        check_vma=False,
    )
```

```python
import functools

import jax
import jax.numpy as jnp
import numpy as np
from jax import lax
from jax.experimental import pallas as pl
from jax.experimental.pallas import tpu as pltpu
from jax.sharding import PartitionSpec as P

stencil_weights = (
    -5369.0 / 1800.0,
    12.0 / 7.0,
    -15.0 / 56.0,
    10.0 / 189.0,
    -1.0 / 112.0,
    2.0 / 1925.0,
    -1.0 / 16632.0,
)
spectrum_center = 8.0
spectrum_half = 8.0
first_ratio = 8.0 / (-0.5 - 8.0)
inverse_two = 2.0 / first_ratio
GROUP = 8
CUTS = 2


def sigma_table(degree):
    sigma_now = jnp.full(degree.shape, first_ratio, jnp.float32)
    for repeat in range(1, 16):
        sigma_now = jnp.where(repeat < degree, 1.0 / (inverse_two - sigma_now), sigma_now)
    sigma_next = 1.0 / (inverse_two - sigma_now)
    sigma_after = 1.0 / (inverse_two - sigma_next)
    return (sigma_now, sigma_next, sigma_after)


def circulant_row(length):
    row = np.zeros(length)
    for m in range(1, len(stencil_weights)):
        row[m % length] += -0.5 * stencil_weights[m]
        row[-m % length] += -0.5 * stencil_weights[m]
    return row


def z_matrix(length):
    row = circulant_row(length)
    full = np.stack([np.roll(row, i) for i in range(length)]).astype(np.float32)
    high = full.astype(jnp.bfloat16)
    low = (full - high.astype(np.float32)).astype(jnp.bfloat16)
    zero = np.zeros_like(high)
    return np.block([[high, low], [high, zero]])


def split(value):
    high = value.astype(jnp.bfloat16)
    low = (value - high.astype(jnp.float32)).astype(jnp.bfloat16)
    return high, low


def kernel(
    sizes,
    root_ref, cur, prev, pot, coef, zmat, out, margin,
    curf, prevf, potf, potb, tcur, tmid, zterm, own, before, chosen, up_in, up_out, down_in, down_out,
    panel, parted, partial, other,
    in_local, in_send, in_recv, back_send, back_recv, pre_send, pre_recv, up_send, up_recv,
    down_send, down_recv, post_send, post_recv, out_sem, sum_send, sum_recv,
):
    orbs, nx, ny, nz, states = sizes
    rows = nx // 2 * ny
    half = orbs // 2 * rows
    groups = orbs // 2 // GROUP
    span = GROUP * rows
    chunks = groups * CUTS
    block = span // CUTS
    dom, state = lax.axis_index("dom"), lax.axis_index("state")
    mate = 1 - dom
    line, b = state // 2, lax.rem(state, 2)
    count = states // 2
    peer = line * 2 + 1 - b

    barrier = pltpu.get_barrier_semaphore()

    def greet(where):
        pl.semaphore_signal(barrier, 1, device_id=where, device_id_type=pl.DeviceIdType.MESH)

    greet({"dom": mate})
    greet({"state": peer})

    @pl.when(line > 0)
    def _():
        greet({"state": state - 2})

    @pl.when(line < count - 1)
    def _():
        greet({"state": state + 2})

    @pl.when(line == 0)
    def _():
        up_in[...] = jnp.zeros_like(up_in)

    @pl.when(line == count - 1)
    def _():
        down_in[...] = jnp.zeros_like(down_in)

    pl.semaphore_wait(barrier, 4 - (line == 0).astype(jnp.int32) - (line == count - 1).astype(jnp.int32))

    def remote(source, target, send, recv, where):
        return pltpu.make_async_remote_copy(
            source, target, send, recv, device_id=where, device_id_type=pl.DeviceIdType.MESH
        )

    here = potf.at[pl.ds(dom * rows, rows)]
    pot_copies = (
        pltpu.make_async_copy(pot, here, in_local.at[2 * groups]),
        remote(pot, here, in_send.at[2 * groups], in_recv.at[2 * groups], {"dom": mate}),
    )

    def coming(g):
        copies = []
        for i, (source, target) in enumerate(((cur, curf), (prev, prevf))):
            here = target.at[pl.ds(dom * half + g * span, span)]
            n = 2 * g + i
            copies.append(
                remote(
                    source.at[pl.ds(mate * half + g * span, span)], here, in_send.at[n], in_recv.at[n], {"dom": mate}
                )
            )
            copies.append(
                pltpu.make_async_copy(source.at[pl.ds(dom * half + g * span, span)], here, in_local.at[n])
            )
        return copies

    for copy in pot_copies:
        copy.start()
    for g in range(groups):
        for copy in coming(g):
            copy.start()
    for copy in pot_copies:
        copy.wait()
    for r in range(2 * rows):
        potb[r] = jnp.broadcast_to(potf[pl.ds(r, 1), :], (GROUP, nz))

    cx, cy = circulant_row(nx), circulant_row(ny)
    centre = -0.5 * 3.0 * stencil_weights[0] + cx[0] + cy[0] - spectrum_center

    def shifted_sum(source, x):
        mid = source[pl.ds(x * ny, ny)]
        acc = zterm[pl.ds(x * ny, ny)] + (centre + potb[pl.ds(x * ny, ny)]) * mid
        for s in range(1, ny // 2 + 1):
            if cy[s]:
                beside = jnp.concatenate([mid[s:], mid[:s]], 0)
                if 2 * s != ny:
                    beside = beside + jnp.concatenate([mid[ny - s:], mid[: ny - s]], 0)
                acc = acc + np.float32(cy[s]) * beside
        for s in range(1, nx // 2 + 1):
            if cx[s]:
                beside = source[pl.ds((x + s) % nx * ny, ny)]
                if 2 * s != nx:
                    beside = beside + source[pl.ds((x - s) % nx * ny, ny)]
                acc = acc + np.float32(cx[s]) * beside
        return acc

    def z_pass(source):
        high, low = split(source[...].reshape(nx * ny * GROUP, nz))
        both = jnp.dot(jnp.concatenate([high, low], 1), zmat[...], preferred_element_type=jnp.float32)
        zterm[...] = (both[:, :nz] + both[:, nz:]).reshape(nx * ny, GROUP, nz)

    def spot(x, y, g):
        slab, r = x // (nx // 2), x % (nx // 2) * ny + y
        return pl.ds(slab * half + g * span + r, GROUP, stride=rows)

    def result_spot(x, y, g):
        slab, r = x // (nx // 2), x % (nx // 2) * ny + y
        start = (2 - dom) * half if slab else dom * 2 * half
        return pl.ds(start + g * span + r, GROUP, stride=rows)

    def back(g):
        return remote(
            own.at[pl.ds(2 * half + g * span, span)], own.at[pl.ds(dom * half + g * span, span)],
            back_send.at[g], back_recv.at[g], {"dom": mate},
        )

    def pre(c):
        return remote(
            own.at[pl.ds((1 - b) * half + c * block, block)], before.at[c],
            pre_send.at[c], pre_recv.at[c], {"state": peer},
        )

    def hand_over(g):
        back(g).wait_recv()
        for i in range(CUTS):
            pre(g * CUTS + i).start()

    def one_group(g, carry):
        for copy in coming(g):
            copy.wait()
        mine = pl.ds(dom * (orbs // 2) + g * GROUP, GROUP)
        for x in range(nx):
            for y in range(ny):
                tcur[x * ny + y] = curf[spot(x, y, g), :]
        z_pass(tcur)
        c1, d1 = coef[0, mine], coef[1, mine]
        for x in range(nx):
            acc = shifted_sum(tcur, x)
            for y in range(ny):
                tmid[x * ny + y] = c1 * acc[y] - d1 * prevf[spot(x, y, g), :]
        z_pass(tmid)
        c2, d2 = coef[2, mine], coef[3, mine]
        for x in range(nx):
            acc = shifted_sum(tmid, x)
            for y in range(ny):
                own[result_spot(x, y, g), :] = c2 * acc[y] - d2 * tcur[x * ny + y]
        back(g).start()

        @pl.when(g > 0)
        def _():
            hand_over(g - 1)

        return carry

    lax.fori_loop(0, groups, one_group, 0)
    hand_over(groups - 1)
    write = pltpu.make_async_copy(own.at[pl.ds(0, 2 * half)], out, out_sem)
    write.start()

    root = root_ref[0]
    root_line, root_b = root // 2, lax.rem(root, 2)

    def up(c):
        return remote(up_out.at[c], up_in.at[c], up_send.at[c], up_recv.at[c], {"state": state + 2})

    def down(c):
        return remote(down_out.at[c], down_in.at[c], down_send.at[c], down_recv.at[c], {"state": state - 2})

    def post(c):
        place = panel.at[pl.ds(b * half + c * block, block)]
        return remote(place, place, post_send.at[c], post_recv.at[c], {"state": peer})

    near = jnp.minimum(line, count - 1 - line)
    far = jnp.maximum(line, count - 1 - line)

    def at_step(c, action):
        @pl.when((c >= 0) & (c < chunks))
        def _():
            action(c)

    def choose(c):
        pre(c).wait_recv()
        chosen[c] = jnp.where(root_b == b, own[pl.ds(b * half + c * block, block), :], before[c])

    def go_up(c):
        @pl.when(line > 0)
        def _():
            up(c).wait_recv()

        @pl.when(line < count - 1)
        def _():
            up_out[c] = jnp.where(root_line == line, chosen[c], up_in[c])
            up(c).start()

    def go_down(c):
        @pl.when(line < count - 1)
        def _():
            down(c).wait_recv()

        @pl.when(line > 0)
        def _():
            down_out[c] = jnp.where(root_line == line, chosen[c], down_in[c])
            down(c).start()

    def finish(c):
        arrived = jnp.where(root_line < line, up_in[c], down_in[c])
        panel[pl.ds(b * half + c * block, block), :] = jnp.where(root_line == line, chosen[c], arrived)
        post(c).start()

    def wave(t, carry):
        at_step(t - near, choose)
        at_step(t - line, go_up)
        at_step(t - (count - 1 - line), go_down)
        at_step(t - far, finish)
        return carry

    lax.fori_loop(0, chunks + count - 1, wave, 0)

    for r in range(rows):
        high, low = split(own[pl.ds(r, orbs, stride=rows), :])
        parted[r] = jnp.concatenate([high, high, low], 1)

    def every(size, action):
        def step(c, carry):
            action(c)
            return carry

        lax.fori_loop(0, size, step, 0)

    def post_in(c):
        place = panel.at[pl.ds((1 - b) * half + c * block, block)]
        return remote(place, place, post_send.at[c], post_recv.at[c], {"state": peer})

    every(chunks, lambda c: post_in(c).wait_recv())

    total = jnp.zeros((orbs, orbs), jnp.float32)
    for r in range(rows):
        high, low = split(panel[pl.ds(r, orbs, stride=rows), :])
        total = total + lax.dot_general(
            jnp.concatenate([high, low, high], 1), parted[r], (((1,), (1,)), ((), ())),
            preferred_element_type=jnp.float32,
        )
    partial[:, :orbs] = total * np.float32(1.0 / (nx * ny * nz))
    share = orbs // 2
    swap = remote(partial.at[pl.ds(mate * share, share)], other, sum_send, sum_recv, {"dom": mate})
    swap.start()
    swap.wait()
    margin[...] = partial[pl.ds(dom * share, share), :orbs] + other[:, :orbs]

    every(groups, lambda g: back(g).wait_send())

    def sent(c):
        pre(c).wait_send()
        post(c).wait_send()

        @pl.when(line < count - 1)
        def _():
            up(c).wait_send()

        @pl.when(line > 0)
        def _():
            down(c).wait_send()

    every(chunks, sent)
    write.wait()


def on_device(mesh, previous, current, potential, degree, panel_index):
    orbs, planes, ny, nz = previous.shape
    states = mesh.shape["state"]
    nx = planes * mesh.shape["dom"]
    rows = planes * ny
    sigma_now, sigma_next, sigma_after = sigma_table(degree)
    table = jnp.stack(
        [
            2.0 * sigma_next / spectrum_half,
            sigma_now * sigma_next,
            2.0 * sigma_after / spectrum_half,
            sigma_next * sigma_after,
        ]
    )
    coef = jnp.broadcast_to(table[:, :, None], (4, orbs, nz))
    zmat = jnp.asarray(z_matrix(nz))
    vmem, anyspace = pl.BlockSpec(memory_space=pltpu.VMEM), pl.BlockSpec(memory_space=pl.ANY)
    f32, bf16 = jnp.float32, jnp.bfloat16
    groups = orbs // 2 // GROUP
    chunks = groups * CUTS
    block = GROUP * rows // CUTS
    dma = pltpu.SemaphoreType.DMA
    filtered, margin = pl.pallas_call(
        functools.partial(kernel, (orbs, nx, ny, nz, states)),
        out_shape=(
            jax.ShapeDtypeStruct((orbs * rows, nz), f32),
            jax.ShapeDtypeStruct((orbs // 2, orbs), f32),
        ),
        in_specs=[pl.BlockSpec(memory_space=pltpu.SMEM), anyspace, anyspace, anyspace, vmem, vmem],
        out_specs=(anyspace, vmem),
        scratch_shapes=[
            pltpu.VMEM((orbs * rows, nz), f32),
            pltpu.VMEM((orbs * rows, nz), f32),
            pltpu.VMEM((nx * ny, nz), f32),
            pltpu.VMEM((nx * ny, GROUP, nz), f32),
            pltpu.VMEM((nx * ny, GROUP, nz), f32),
            pltpu.VMEM((nx * ny, GROUP, nz), f32),
            pltpu.VMEM((nx * ny, GROUP, nz), f32),
            pltpu.VMEM((orbs * rows * 3 // 2, nz), f32),
            *[pltpu.VMEM((chunks, block, nz), f32)] * 6,
            pltpu.VMEM((orbs * rows, nz), f32),
            pltpu.VMEM((rows, orbs, 3 * nz), bf16),
            pltpu.VMEM((orbs, 128), f32),
            pltpu.VMEM((orbs // 2, 128), f32),
            *[dma((2 * groups + 1,))] * 3,
            *[dma((groups,))] * 2,
            *[dma((chunks,))] * 8,
            dma, dma, dma,
        ],
        compiler_params=pltpu.CompilerParams(
            collective_id=0, has_side_effects=True, vmem_limit_bytes=60 * 1024 * 1024
        ),
    )(
        panel_index,
        current.reshape(orbs * rows, nz),
        previous.reshape(orbs * rows, nz),
        potential.reshape(rows, nz),
        coef,
        zmat,
    )
    return filtered.reshape(previous.shape), margin


def solution(mesh):
    return jax.shard_map(
        functools.partial(on_device, mesh),
        mesh=mesh,
        in_specs=(
            P(("kpt", "state"), "dom", None, None),
            P(("kpt", "state"), "dom", None, None),
            P("dom", None, None),
            P(("kpt", "state")),
            P("kpt"),
        ),
        out_specs=(P(("kpt", "state"), "dom", None, None), P(("kpt", "dom"), "state")),
        check_vma=False,
    )
```

```python
import functools

import jax
import jax.numpy as jnp
import numpy as np
from jax import lax
from jax.experimental import pallas as pl
from jax.experimental.pallas import tpu as pltpu
from jax.sharding import PartitionSpec as P

stencil_weights = (
    -5369.0 / 1800.0,
    12.0 / 7.0,
    -15.0 / 56.0,
    10.0 / 189.0,
    -1.0 / 112.0,
    2.0 / 1925.0,
    -1.0 / 16632.0,
)
spectrum_center = 8.0
spectrum_half = 8.0
first_ratio = 8.0 / (-0.5 - 8.0)
inverse_two = 2.0 / first_ratio
GROUP = 8
CUTS = 2
SKEW = 3


def sigma_table(degree):
    sigma_now = jnp.full(degree.shape, first_ratio, jnp.float32)
    for repeat in range(1, 16):
        sigma_now = jnp.where(repeat < degree, 1.0 / (inverse_two - sigma_now), sigma_now)
    sigma_next = 1.0 / (inverse_two - sigma_now)
    sigma_after = 1.0 / (inverse_two - sigma_next)
    return (sigma_now, sigma_next, sigma_after)


def circulant_row(length):
    row = np.zeros(length)
    for m in range(1, len(stencil_weights)):
        row[m % length] += -0.5 * stencil_weights[m]
        row[-m % length] += -0.5 * stencil_weights[m]
    return row


def split(value):
    high = value.astype(jnp.bfloat16)
    low = (value - high.astype(jnp.float32)).astype(jnp.bfloat16)
    return high, low


def fill_z_matrix(zmat, length):
    row = circulant_row(length)
    shape = (length, length)
    apart = lax.broadcasted_iota(jnp.int32, shape, 0) - lax.broadcasted_iota(jnp.int32, shape, 1)
    apart = jnp.where(apart < 0, apart + length, apart)
    full = jnp.zeros(shape, jnp.float32)
    for s in range(length):
        if row[s]:
            full = jnp.where(apart == s, np.float32(row[s]), full)
    high, low = split(full)
    top = jnp.concatenate([high, low], 1)
    zmat[...] = jnp.concatenate([top, jnp.concatenate([high, jnp.zeros_like(low)], 1)], 0)


def fill_coefficients(coef, degree, width):
    now, following, after = sigma_table(degree)
    orbs = degree.shape[1]
    shape = (orbs, orbs)
    diagonal = lax.broadcasted_iota(jnp.int32, shape, 0) == lax.broadcasted_iota(jnp.int32, shape, 1)
    for i, line in enumerate(
        (2.0 * following / spectrum_half, now * following, 2.0 * after / spectrum_half, following * after)
    ):
        column = jnp.sum(jnp.where(diagonal, jnp.broadcast_to(line, shape), 0.0), axis=1, keepdims=True)
        coef[i] = jnp.broadcast_to(column, (orbs, width))


def kernel(
    sizes,
    root_ref, degree, cur, prev, pot, out, margin, coef, zmat,
    curf, prevf, potf, potb, tcur, tmid, zterm, own, before, chosen, up_in, up_out, down_in, down_out,
    panel, parted, partial, other,
    in_local, in_send, in_recv, back_send, back_recv, pre_send, pre_recv, up_send, up_recv,
    down_send, down_recv, post_send, post_recv, out_sem, sum_send, sum_recv,
):
    orbs, nx, ny, nz, states = sizes
    rows = nx // 2 * ny
    half = orbs // 2 * rows
    groups = orbs // 2 // GROUP
    span = GROUP * rows
    chunks = groups * CUTS
    block = span // CUTS
    dom, state = lax.axis_index("dom"), lax.axis_index("state")
    mate = 1 - dom
    line, b = state // 2, lax.rem(state, 2)
    count = states // 2
    peer = line * 2 + 1 - b

    barrier = pltpu.get_barrier_semaphore()

    def greet(where):
        pl.semaphore_signal(barrier, 1, device_id=where, device_id_type=pl.DeviceIdType.MESH)

    greet({"dom": mate})
    greet({"state": peer})

    @pl.when(line > 0)
    def _():
        greet({"state": state - 2})

    @pl.when(line < count - 1)
    def _():
        greet({"state": state + 2})

    @pl.when(line == 0)
    def _():
        up_in[...] = jnp.zeros_like(up_in)

    @pl.when(line == count - 1)
    def _():
        down_in[...] = jnp.zeros_like(down_in)

    fill_z_matrix(zmat, nz)
    pl.semaphore_wait(barrier, 4 - (line == 0).astype(jnp.int32) - (line == count - 1).astype(jnp.int32))

    def remote(source, target, send, recv, where):
        return pltpu.make_async_remote_copy(
            source, target, send, recv, device_id=where, device_id_type=pl.DeviceIdType.MESH
        )

    here = potf.at[pl.ds(dom * rows, rows)]
    pot_copies = (
        pltpu.make_async_copy(pot, here, in_local.at[2 * groups]),
        remote(pot, here, in_send.at[2 * groups], in_recv.at[2 * groups], {"dom": mate}),
    )

    def coming(g):
        copies = []
        for i, (source, target) in enumerate(((cur, curf), (prev, prevf))):
            here = target.at[pl.ds(dom * half + g * span, span)]
            n = 2 * g + i
            copies.append(
                remote(
                    source.at[pl.ds(mate * half + g * span, span)], here, in_send.at[n], in_recv.at[n], {"dom": mate}
                )
            )
            copies.append(
                pltpu.make_async_copy(source.at[pl.ds(dom * half + g * span, span)], here, in_local.at[n])
            )
        return copies

    for copy in pot_copies:
        copy.start()
    for g in range(groups):
        for copy in coming(g):
            copy.start()
    fill_coefficients(coef, degree[...], nz)
    for copy in pot_copies:
        copy.wait()
    for r in range(2 * rows):
        potb[r] = jnp.broadcast_to(potf[pl.ds(r, 1), :], (GROUP, nz))

    cx, cy = circulant_row(nx), circulant_row(ny)
    centre = -0.5 * 3.0 * stencil_weights[0] + cx[0] + cy[0] - spectrum_center

    def shifted_sum(source, x):
        mid = source[pl.ds(x * ny, ny)]
        acc = zterm[pl.ds(x * ny, ny)] + (centre + potb[pl.ds(x * ny, ny)]) * mid
        for s in range(1, ny // 2 + 1):
            if cy[s]:
                beside = jnp.concatenate([mid[s:], mid[:s]], 0)
                if 2 * s != ny:
                    beside = beside + jnp.concatenate([mid[ny - s:], mid[: ny - s]], 0)
                acc = acc + np.float32(cy[s]) * beside
        for s in range(1, nx // 2 + 1):
            if cx[s]:
                beside = source[pl.ds((x + s) % nx * ny, ny)]
                if 2 * s != nx:
                    beside = beside + source[pl.ds((x - s) % nx * ny, ny)]
                acc = acc + np.float32(cx[s]) * beside
        return acc

    def z_pass(source):
        high, low = split(source[...].reshape(nx * ny * GROUP, nz))
        both = jnp.dot(jnp.concatenate([high, low], 1), zmat[...], preferred_element_type=jnp.float32)
        zterm[...] = (both[:, :nz] + both[:, nz:]).reshape(nx * ny, GROUP, nz)

    def spot(x, y, g):
        slab, r = x // (nx // 2), x % (nx // 2) * ny + y
        return pl.ds(slab * half + g * span + r, GROUP, stride=rows)

    def result_spot(x, y, g):
        slab, r = x // (nx // 2), x % (nx // 2) * ny + y
        start = (2 - dom) * half if slab else dom * 2 * half
        return pl.ds(start + g * span + r, GROUP, stride=rows)

    def back(g):
        return remote(
            own.at[pl.ds(2 * half + g * span, span)], own.at[pl.ds(dom * half + g * span, span)],
            back_send.at[g], back_recv.at[g], {"dom": mate},
        )

    def pre(c):
        return remote(
            own.at[pl.ds((1 - b) * half + c * block, block)], before.at[c],
            pre_send.at[c], pre_recv.at[c], {"state": peer},
        )

    def hand_over(g):
        for i in range(CUTS):
            pre(g * CUTS + i).start()

    def one_group(g, carry):
        for copy in coming(g):
            copy.wait()
        mine = pl.ds(dom * (orbs // 2) + g * GROUP, GROUP)
        for x in range(nx):
            for y in range(ny):
                tcur[x * ny + y] = curf[spot(x, y, g), :]
        z_pass(tcur)
        c1, d1 = coef[0, mine], coef[1, mine]
        for x in range(nx):
            acc = shifted_sum(tcur, x)
            for y in range(ny):
                tmid[x * ny + y] = c1 * acc[y] - d1 * prevf[spot(x, y, g), :]
        z_pass(tmid)
        c2, d2 = coef[2, mine], coef[3, mine]
        for x in range(nx):
            acc = shifted_sum(tmid, x)
            for y in range(ny):
                own[result_spot(x, y, g), :] = c2 * acc[y] - d2 * tcur[x * ny + y]
        back(g).start()

        @pl.when(dom != b)
        def _():
            hand_over(g)

        @pl.when((dom == b) & (g > 0))
        def _():
            back(g - 1).wait_recv()
            hand_over(g - 1)

        return carry

    lax.fori_loop(0, groups, one_group, 0)

    @pl.when(dom == b)
    def _():
        back(groups - 1).wait_recv()
        hand_over(groups - 1)

    @pl.when(dom != b)
    def _():
        for g in range(groups):
            back(g).wait_recv()

    write = pltpu.make_async_copy(own.at[pl.ds(0, 2 * half)], out, out_sem)
    write.start()

    root = root_ref[0]
    root_line, root_b = root // 2, lax.rem(root, 2)

    def up(c):
        return remote(up_out.at[c], up_in.at[c], up_send.at[c], up_recv.at[c], {"state": state + 2})

    def down(c):
        return remote(down_out.at[c], down_in.at[c], down_send.at[c], down_recv.at[c], {"state": state - 2})

    def post(c):
        place = panel.at[pl.ds(b * half + c * block, block)]
        return remote(place, place, post_send.at[c], post_recv.at[c], {"state": peer})

    below, above = SKEW * line, SKEW * (count - 1 - line)
    near, far = jnp.minimum(below, above), jnp.maximum(below, above)

    def at_step(c, action):
        @pl.when((c >= 0) & (c < chunks))
        def _():
            action(c)

    def choose(c):
        pre(c).wait_recv()
        chosen[c] = jnp.where(root_b == b, own[pl.ds(b * half + c * block, block), :], before[c])

    def go_up(c):
        @pl.when(line > 0)
        def _():
            up(c).wait_recv()

        @pl.when(line < count - 1)
        def _():
            up_out[c] = jnp.where(root_line == line, chosen[c], up_in[c])
            up(c).start()

    def go_down(c):
        @pl.when(line < count - 1)
        def _():
            down(c).wait_recv()

        @pl.when(line > 0)
        def _():
            down_out[c] = jnp.where(root_line == line, chosen[c], down_in[c])
            down(c).start()

    def finish(c):
        arrived = jnp.where(root_line < line, up_in[c], down_in[c])
        panel[pl.ds(b * half + c * block, block), :] = jnp.where(root_line == line, chosen[c], arrived)
        post(c).start()

    def wave(t, carry):
        at_step(t - near, choose)
        at_step(t - below, go_up)
        at_step(t - above, go_down)
        at_step(t - far, finish)
        return carry

    lax.fori_loop(0, chunks + SKEW * (count - 1), wave, 0)

    for r in range(rows):
        high, low = split(own[pl.ds(r, orbs, stride=rows), :])
        parted[r] = jnp.concatenate([high, high, low], 1)

    def every(size, action):
        def step(c, carry):
            action(c)
            return carry

        lax.fori_loop(0, size, step, 0)

    def post_in(c):
        place = panel.at[pl.ds((1 - b) * half + c * block, block)]
        return remote(place, place, post_send.at[c], post_recv.at[c], {"state": peer})

    every(chunks, lambda c: post_in(c).wait_recv())

    total = jnp.zeros((orbs, orbs), jnp.float32)
    for r in range(rows):
        high, low = split(panel[pl.ds(r, orbs, stride=rows), :])
        total = total + lax.dot_general(
            jnp.concatenate([high, low, high], 1), parted[r], (((1,), (1,)), ((), ())),
            preferred_element_type=jnp.float32,
        )
    partial[:, :orbs] = total * np.float32(1.0 / (nx * ny * nz))
    share = orbs // 2
    swap = remote(partial.at[pl.ds(mate * share, share)], other, sum_send, sum_recv, {"dom": mate})
    swap.start()
    swap.wait()
    margin[...] = partial[pl.ds(dom * share, share), :orbs] + other[:, :orbs]

    every(groups, lambda g: back(g).wait_send())

    def sent(c):
        pre(c).wait_send()
        post(c).wait_send()

        @pl.when(line < count - 1)
        def _():
            up(c).wait_send()

        @pl.when(line > 0)
        def _():
            down(c).wait_send()

    every(chunks, sent)
    write.wait()


def on_device(mesh, previous, current, potential, degree, panel_index):
    orbs, planes, ny, nz = previous.shape
    states = mesh.shape["state"]
    nx = planes * mesh.shape["dom"]
    rows = planes * ny
    vmem, anyspace = pl.BlockSpec(memory_space=pltpu.VMEM), pl.BlockSpec(memory_space=pl.ANY)
    hbm = pl.BlockSpec(memory_space=pltpu.HBM)
    f32, bf16 = jnp.float32, jnp.bfloat16
    groups = orbs // 2 // GROUP
    chunks = groups * CUTS
    block = GROUP * rows // CUTS
    dma = pltpu.SemaphoreType.DMA
    filtered, margin = pl.pallas_call(
        functools.partial(kernel, (orbs, nx, ny, nz, states)),
        out_shape=(
            jax.ShapeDtypeStruct((orbs * rows, nz), f32),
            jax.ShapeDtypeStruct((orbs // 2, orbs), f32),
        ),
        in_specs=[pl.BlockSpec(memory_space=pltpu.SMEM), vmem, hbm, hbm, hbm],
        out_specs=(anyspace, vmem),
        scratch_shapes=[
            pltpu.VMEM((4, orbs, nz), f32),
            pltpu.VMEM((2 * nz, 2 * nz), bf16),
            pltpu.VMEM((orbs * rows, nz), f32),
            pltpu.VMEM((orbs * rows, nz), f32),
            pltpu.VMEM((nx * ny, nz), f32),
            pltpu.VMEM((nx * ny, GROUP, nz), f32),
            pltpu.VMEM((nx * ny, GROUP, nz), f32),
            pltpu.VMEM((nx * ny, GROUP, nz), f32),
            pltpu.VMEM((nx * ny, GROUP, nz), f32),
            pltpu.VMEM((orbs * rows * 3 // 2, nz), f32),
            *[pltpu.VMEM((chunks, block, nz), f32)] * 6,
            pltpu.VMEM((orbs * rows, nz), f32),
            pltpu.VMEM((rows, orbs, 3 * nz), bf16),
            pltpu.VMEM((orbs, 128), f32),
            pltpu.VMEM((orbs // 2, 128), f32),
            *[dma((2 * groups + 1,))] * 3,
            *[dma((groups,))] * 2,
            *[dma((chunks,))] * 8,
            dma, dma, dma,
        ],
        compiler_params=pltpu.CompilerParams(
            collective_id=0, has_side_effects=True, vmem_limit_bytes=60 * 1024 * 1024
        ),
    )(
        panel_index,
        degree.reshape(1, orbs),
        current.reshape(orbs * rows, nz),
        previous.reshape(orbs * rows, nz),
        potential.reshape(rows, nz),
    )
    return filtered.reshape(previous.shape), margin


def solution(mesh):
    return jax.shard_map(
        functools.partial(on_device, mesh),
        mesh=mesh,
        in_specs=(
            P(("kpt", "state"), "dom", None, None),
            P(("kpt", "state"), "dom", None, None),
            P("dom", None, None),
            P(("kpt", "state")),
            P("kpt"),
        ),
        out_specs=(P(("kpt", "state"), "dom", None, None), P(("kpt", "dom"), "state")),
        check_vma=False,
    )
```

```python
import functools

import jax
import jax.numpy as jnp
import numpy as np
from jax import lax
from jax.experimental import pallas as pl
from jax.experimental.pallas import tpu as pltpu
from jax.sharding import PartitionSpec as P

stencil_weights = (
    -5369.0 / 1800.0,
    12.0 / 7.0,
    -15.0 / 56.0,
    10.0 / 189.0,
    -1.0 / 112.0,
    2.0 / 1925.0,
    -1.0 / 16632.0,
)
spectrum_center = 8.0
spectrum_half = 8.0
first_ratio = 8.0 / (-0.5 - 8.0)
inverse_two = 2.0 / first_ratio
GROUP = 8
CUTS = 4
SKEW = 5


def sigma_table(degree):
    sigma_now = jnp.full(degree.shape, first_ratio, jnp.float32)
    for repeat in range(1, 16):
        sigma_now = jnp.where(repeat < degree, 1.0 / (inverse_two - sigma_now), sigma_now)
    sigma_next = 1.0 / (inverse_two - sigma_now)
    sigma_after = 1.0 / (inverse_two - sigma_next)
    return (sigma_now, sigma_next, sigma_after)


def circulant_row(length):
    row = np.zeros(length)
    for m in range(1, len(stencil_weights)):
        row[m % length] += -0.5 * stencil_weights[m]
        row[-m % length] += -0.5 * stencil_weights[m]
    return row


def split(value):
    high = value.astype(jnp.bfloat16)
    low = (value - high.astype(jnp.float32)).astype(jnp.bfloat16)
    return high, low


def fill_z_matrix(zmat, length):
    row = circulant_row(length)
    shape = (length, length)
    apart = lax.broadcasted_iota(jnp.int32, shape, 0) - lax.broadcasted_iota(jnp.int32, shape, 1)
    apart = jnp.where(apart < 0, apart + length, apart)
    full = jnp.zeros(shape, jnp.float32)
    for s in range(length):
        if row[s]:
            full = jnp.where(apart == s, np.float32(row[s]), full)
    high, low = split(full)
    top = jnp.concatenate([high, low], 1)
    zmat[...] = jnp.concatenate([top, jnp.concatenate([high, jnp.zeros_like(low)], 1)], 0)


def fill_coefficients(coef, degree, width):
    now, following, after = sigma_table(degree)
    orbs = degree.shape[1]
    shape = (orbs, orbs)
    diagonal = lax.broadcasted_iota(jnp.int32, shape, 0) == lax.broadcasted_iota(jnp.int32, shape, 1)
    for i, line in enumerate(
        (2.0 * following / spectrum_half, now * following, 2.0 * after / spectrum_half, following * after)
    ):
        column = jnp.sum(jnp.where(diagonal, jnp.broadcast_to(line, shape), 0.0), axis=1, keepdims=True)
        coef[i] = jnp.broadcast_to(column, (orbs, width))


def kernel(
    sizes,
    root_ref, degree, cur, prev, pot, out, margin, coef, zmat,
    curf, prevf, potf, potb, tcur, tmid, zterm, own, before, chosen, up_in, up_out, down_in, down_out,
    panel, parted, partial, other,
    in_local, in_send, in_recv, back_send, back_recv, pre_send, pre_recv, up_send, up_recv,
    down_send, down_recv, post_send, post_recv, out_sem, sum_send, sum_recv,
):
    orbs, nx, ny, nz, states = sizes
    rows = nx // 2 * ny
    half = orbs // 2 * rows
    groups = orbs // 2 // GROUP
    span = GROUP * rows
    chunks = groups * CUTS
    block = span // CUTS
    dom, state = lax.axis_index("dom"), lax.axis_index("state")
    mate = 1 - dom
    line, b = state // 2, lax.rem(state, 2)
    count = states // 2
    peer = line * 2 + 1 - b

    barrier = pltpu.get_barrier_semaphore()

    def greet(where):
        pl.semaphore_signal(barrier, 1, device_id=where, device_id_type=pl.DeviceIdType.MESH)

    greet({"dom": mate})
    greet({"state": peer})

    @pl.when(line > 0)
    def _():
        greet({"state": state - 2})

    @pl.when(line < count - 1)
    def _():
        greet({"state": state + 2})

    @pl.when(line == 0)
    def _():
        up_in[...] = jnp.zeros_like(up_in)

    @pl.when(line == count - 1)
    def _():
        down_in[...] = jnp.zeros_like(down_in)

    fill_z_matrix(zmat, nz)
    pl.semaphore_wait(barrier, 4 - (line == 0).astype(jnp.int32) - (line == count - 1).astype(jnp.int32))

    def remote(source, target, send, recv, where):
        return pltpu.make_async_remote_copy(
            source, target, send, recv, device_id=where, device_id_type=pl.DeviceIdType.MESH
        )

    here = potf.at[pl.ds(dom * rows, rows)]
    pot_copies = (
        pltpu.make_async_copy(pot, here, in_local.at[2 * groups]),
        remote(pot, here, in_send.at[2 * groups], in_recv.at[2 * groups], {"dom": mate}),
    )

    def coming(g):
        copies = []
        for i, (source, target) in enumerate(((cur, curf), (prev, prevf))):
            here = target.at[pl.ds(dom * half + g * span, span)]
            n = 2 * g + i
            copies.append(
                remote(
                    source.at[pl.ds(mate * half + g * span, span)], here, in_send.at[n], in_recv.at[n], {"dom": mate}
                )
            )
            copies.append(
                pltpu.make_async_copy(source.at[pl.ds(dom * half + g * span, span)], here, in_local.at[n])
            )
        return copies

    for copy in pot_copies:
        copy.start()
    for g in range(groups):
        for copy in coming(g):
            copy.start()
    fill_coefficients(coef, degree[...], nz)
    for copy in pot_copies:
        copy.wait()
    for r in range(2 * rows):
        potb[r] = jnp.broadcast_to(potf[pl.ds(r, 1), :], (GROUP, nz))

    cx, cy = circulant_row(nx), circulant_row(ny)
    centre = -0.5 * 3.0 * stencil_weights[0] + cx[0] + cy[0] - spectrum_center

    def shifted_sum(source, x):
        mid = source[pl.ds(x * ny, ny)]
        acc = zterm[pl.ds(x * ny, ny)] + (centre + potb[pl.ds(x * ny, ny)]) * mid
        for s in range(1, ny // 2 + 1):
            if cy[s]:
                beside = jnp.concatenate([mid[s:], mid[:s]], 0)
                if 2 * s != ny:
                    beside = beside + jnp.concatenate([mid[ny - s:], mid[: ny - s]], 0)
                acc = acc + np.float32(cy[s]) * beside
        for s in range(1, nx // 2 + 1):
            if cx[s]:
                beside = source[pl.ds((x + s) % nx * ny, ny)]
                if 2 * s != nx:
                    beside = beside + source[pl.ds((x - s) % nx * ny, ny)]
                acc = acc + np.float32(cx[s]) * beside
        return acc

    def z_pass(source):
        high, low = split(source[...].reshape(nx * ny * GROUP, nz))
        both = jnp.dot(jnp.concatenate([high, low], 1), zmat[...], preferred_element_type=jnp.float32)
        zterm[...] = (both[:, :nz] + both[:, nz:]).reshape(nx * ny, GROUP, nz)

    def spot(x, y, g):
        slab, r = x // (nx // 2), x % (nx // 2) * ny + y
        return pl.ds(slab * half + g * span + r, GROUP, stride=rows)

    def result_spot(x, y, g):
        slab, r = x // (nx // 2), x % (nx // 2) * ny + y
        start = (2 - dom) * half if slab else dom * 2 * half
        return pl.ds(start + g * span + r, GROUP, stride=rows)

    def back(g):
        return remote(
            own.at[pl.ds(2 * half + g * span, span)], own.at[pl.ds(dom * half + g * span, span)],
            back_send.at[g], back_recv.at[g], {"dom": mate},
        )

    def pre(c):
        return remote(
            own.at[pl.ds((1 - b) * half + c * block, block)], before.at[c],
            pre_send.at[c], pre_recv.at[c], {"state": peer},
        )

    def hand_over(g):
        for i in range(CUTS):
            pre(g * CUTS + i).start()

    def one_group(g, carry):
        for copy in coming(g):
            copy.wait()
        mine = pl.ds(dom * (orbs // 2) + g * GROUP, GROUP)
        for x in range(nx):
            for y in range(ny):
                tcur[x * ny + y] = curf[spot(x, y, g), :]
        z_pass(tcur)
        c1, d1 = coef[0, mine], coef[1, mine]
        for x in range(nx):
            acc = shifted_sum(tcur, x)
            for y in range(ny):
                tmid[x * ny + y] = c1 * acc[y] - d1 * prevf[spot(x, y, g), :]
        z_pass(tmid)
        c2, d2 = coef[2, mine], coef[3, mine]
        for x in range(nx):
            acc = shifted_sum(tmid, x)
            for y in range(ny):
                own[result_spot(x, y, g), :] = c2 * acc[y] - d2 * tcur[x * ny + y]
        back(g).start()

        @pl.when(dom != b)
        def _():
            hand_over(g)

        @pl.when((dom == b) & (g > 0))
        def _():
            back(g - 1).wait_recv()
            hand_over(g - 1)

        return carry

    lax.fori_loop(0, groups, one_group, 0)

    @pl.when(dom == b)
    def _():
        back(groups - 1).wait_recv()
        hand_over(groups - 1)

    @pl.when(dom != b)
    def _():
        for g in range(groups):
            back(g).wait_recv()

    write = pltpu.make_async_copy(own.at[pl.ds(0, 2 * half)], out, out_sem)
    write.start()

    root = root_ref[0]
    root_line, root_b = root // 2, lax.rem(root, 2)

    def up(c):
        return remote(up_out.at[c], up_in.at[c], up_send.at[c], up_recv.at[c], {"state": state + 2})

    def down(c):
        return remote(down_out.at[c], down_in.at[c], down_send.at[c], down_recv.at[c], {"state": state - 2})

    def post(c):
        place = panel.at[pl.ds(b * half + c * block, block)]
        return remote(place, place, post_send.at[c], post_recv.at[c], {"state": peer})

    below, above = SKEW * line, SKEW * (count - 1 - line)
    near, far = jnp.minimum(below, above), jnp.maximum(below, above)

    def at_step(c, action):
        @pl.when((c >= 0) & (c < chunks))
        def _():
            action(c)

    def choose(c):
        pre(c).wait_recv()
        chosen[c] = jnp.where(root_b == b, own[pl.ds(b * half + c * block, block), :], before[c])

    def go_up(c):
        @pl.when(line > 0)
        def _():
            up(c).wait_recv()

        @pl.when(line < count - 1)
        def _():
            up_out[c] = jnp.where(root_line == line, chosen[c], up_in[c])
            up(c).start()

    def go_down(c):
        @pl.when(line < count - 1)
        def _():
            down(c).wait_recv()

        @pl.when(line > 0)
        def _():
            down_out[c] = jnp.where(root_line == line, chosen[c], down_in[c])
            down(c).start()

    def finish(c):
        arrived = jnp.where(root_line < line, up_in[c], down_in[c])
        panel[pl.ds(b * half + c * block, block), :] = jnp.where(root_line == line, chosen[c], arrived)
        post(c).start()

    def wave(t, carry):
        at_step(t - near, choose)
        at_step(t - below, go_up)
        at_step(t - above, go_down)
        at_step(t - far, finish)
        return carry

    lax.fori_loop(0, chunks + SKEW * (count - 1), wave, 0)

    for r in range(rows):
        high, low = split(own[pl.ds(r, orbs, stride=rows), :])
        parted[r] = jnp.concatenate([high, high, low], 1)

    def every(size, action):
        def step(c, carry):
            action(c)
            return carry

        lax.fori_loop(0, size, step, 0)

    def post_in(c):
        place = panel.at[pl.ds((1 - b) * half + c * block, block)]
        return remote(place, place, post_send.at[c], post_recv.at[c], {"state": peer})

    def products(which):
        total = jnp.zeros((orbs // 2, orbs), jnp.float32)
        for r in range(rows):
            high, low = split(panel[pl.ds(which * half + r, orbs // 2, stride=rows), :])
            total = total + lax.dot_general(
                jnp.concatenate([high, low, high], 1), parted[r], (((1,), (1,)), ((), ())),
                preferred_element_type=jnp.float32,
            )
        partial[pl.ds(which * (orbs // 2), orbs // 2), :orbs] = total * np.float32(1.0 / (nx * ny * nz))

    products(b)
    every(chunks, lambda c: post_in(c).wait_recv())
    products(1 - b)
    share = orbs // 2
    swap = remote(partial.at[pl.ds(mate * share, share)], other, sum_send, sum_recv, {"dom": mate})
    swap.start()
    swap.wait()
    margin[...] = partial[pl.ds(dom * share, share), :orbs] + other[:, :orbs]

    every(groups, lambda g: back(g).wait_send())

    def sent(c):
        pre(c).wait_send()
        post(c).wait_send()

        @pl.when(line < count - 1)
        def _():
            up(c).wait_send()

        @pl.when(line > 0)
        def _():
            down(c).wait_send()

    every(chunks, sent)
    write.wait()


def on_device(mesh, previous, current, potential, degree, panel_index):
    orbs, planes, ny, nz = previous.shape
    states = mesh.shape["state"]
    nx = planes * mesh.shape["dom"]
    rows = planes * ny
    vmem, anyspace = pl.BlockSpec(memory_space=pltpu.VMEM), pl.BlockSpec(memory_space=pl.ANY)
    hbm = pl.BlockSpec(memory_space=pltpu.HBM)
    f32, bf16 = jnp.float32, jnp.bfloat16
    groups = orbs // 2 // GROUP
    chunks = groups * CUTS
    block = GROUP * rows // CUTS
    dma = pltpu.SemaphoreType.DMA
    filtered, margin = pl.pallas_call(
        functools.partial(kernel, (orbs, nx, ny, nz, states)),
        out_shape=(
            jax.ShapeDtypeStruct((orbs * rows, nz), f32),
            jax.ShapeDtypeStruct((orbs // 2, orbs), f32),
        ),
        in_specs=[pl.BlockSpec(memory_space=pltpu.SMEM), vmem, hbm, hbm, hbm],
        out_specs=(anyspace, vmem),
        scratch_shapes=[
            pltpu.VMEM((4, orbs, nz), f32),
            pltpu.VMEM((2 * nz, 2 * nz), bf16),
            pltpu.VMEM((orbs * rows, nz), f32),
            pltpu.VMEM((orbs * rows, nz), f32),
            pltpu.VMEM((nx * ny, nz), f32),
            pltpu.VMEM((nx * ny, GROUP, nz), f32),
            pltpu.VMEM((nx * ny, GROUP, nz), f32),
            pltpu.VMEM((nx * ny, GROUP, nz), f32),
            pltpu.VMEM((nx * ny, GROUP, nz), f32),
            pltpu.VMEM((orbs * rows * 3 // 2, nz), f32),
            *[pltpu.VMEM((chunks, block, nz), f32)] * 6,
            pltpu.VMEM((orbs * rows, nz), f32),
            pltpu.VMEM((rows, orbs, 3 * nz), bf16),
            pltpu.VMEM((orbs, 128), f32),
            pltpu.VMEM((orbs // 2, 128), f32),
            *[dma((2 * groups + 1,))] * 3,
            *[dma((groups,))] * 2,
            *[dma((chunks,))] * 8,
            dma, dma, dma,
        ],
        compiler_params=pltpu.CompilerParams(
            collective_id=0, has_side_effects=True, vmem_limit_bytes=60 * 1024 * 1024
        ),
    )(
        panel_index,
        degree.reshape(1, orbs),
        current.reshape(orbs * rows, nz),
        previous.reshape(orbs * rows, nz),
        potential.reshape(rows, nz),
    )
    return filtered.reshape(previous.shape), margin


def solution(mesh):
    return jax.shard_map(
        functools.partial(on_device, mesh),
        mesh=mesh,
        in_specs=(
            P(("kpt", "state"), "dom", None, None),
            P(("kpt", "state"), "dom", None, None),
            P("dom", None, None),
            P(("kpt", "state")),
            P("kpt"),
        ),
        out_specs=(P(("kpt", "state"), "dom", None, None), P(("kpt", "dom"), "state")),
        check_vma=False,
    )
```
